256 devices in a mesh: section: 32 (over z, x_hi, core), tensor: 8 (over x_lo, y).
Axes of the slice: x: 4 (x_hi: 2, x_lo: 2; x = x_hi * 2 + x_lo), y: 4, z: 8, core: 2. Of those that a mesh axis runs over, the one named last changes fastest.
Arguments:
- tokens: bfloat16 [512, 16384], P(None, 'tensor'), may hold values from -6 to 6
- gain: float32 [8, 16384], P(None, 'tensor'), may hold values from 0.25 to 1.75
- w_down: bfloat16 [32, 16384, 64], P('section', 'tensor'), may hold values from -0.046875 to 0.046875
- w_up: bfloat16 [32, 64, 16384], P('section', None, 'tensor'), may hold values from -0.375 to 0.375
- w_value: float32 [16384], P('tensor'), may hold values from -0.046875 to 0.046875
- targets: int32 [512], replicated, may hold values from -128 to 127
Outputs:
- grad_down: bfloat16 [32, 16384, 64], P('section', 'tensor')
- grad_up: bfloat16 [32, 64, 16384], P('section', None, 'tensor')
The draws below stay inside these ranges and needn't reach their ends.
All inputs are finite; a program needn't handle non-finite values.
Results may differ from the reference program's by a relative error of at most 0.022.
Values may be sent and summed in bfloat16 or wider, within the bound.
No kernel may reach another device: no remote copies, remote signals or barrier semaphores. Data moves between devices by JAX's collectives and lax.ppermute only.
A program may use at most 64 MiB of HBM per device.

```python
import jax
import jax.numpy as jnp
from jax import lax

D = 16384
RANK = 256
REPLICAS = 4
LAYERS = 8
TOKENS = 512


def with_ends(entries, rng, low, high):
    spot = [jax.random.randint(jax.random.fold_in(rng, axis), (), 0, length) for axis, length in enumerate(entries.shape)]
    widest = entries.shape.index(max(entries.shape))
    next_to = spot[:widest] + [(spot[widest] + 1) % entries.shape[widest]] + spot[widest + 1:]
    return entries.at[tuple(spot)].set(low).at[tuple(next_to)].set(high)


def steps_of(stream_key, shape, shards, smallest, top_value):
    level, own = 1.0, jax.random.fold_in(stream_key, 6)
    for position, blocks in shards:
        steps = jnp.exp(jax.random.uniform(jax.random.fold_in(own, position), (blocks,), jnp.float32, smallest / len(shards), top_value / len(shards)))
        level = level * jnp.repeat(steps, shape[position] // blocks).reshape([-1 if axis == position else 1 for axis in range(len(shape))])
    return level


def gaussian(stream_key, dims, spread, most, cuts=(), dtype=jnp.bfloat16):
    drawn = jax.random.normal(stream_key, dims, jnp.float32) * spread
    if len(cuts) > 0:
        drawn = steps_of(stream_key, dims, cuts, -0.22, 0.18) * drawn
    return jnp.clip(drawn, min=-most, max=most).astype(dtype)


def setup_inputs(seed: int = 0) -> dict:
    keys = jax.random.split(jax.random.key(seed), 7)
    return {
        "tokens": gaussian(keys[0], (TOKENS, D), 1.0, 6.0, ((1, 8),)),
        "gain": jnp.clip(1.0 + 0.15 * jax.random.normal(keys[1], (LAYERS, D), jnp.float32), 0.25, 1.75),
        "w_down": gaussian(keys[2], (REPLICAS * LAYERS, D, RANK // REPLICAS), D ** -0.5, 0.046875, ((0, 32), (1, 8))),
        "w_up": gaussian(keys[3], (REPLICAS * LAYERS, RANK // REPLICAS, D), RANK ** -0.5, 0.375, ((0, 32), (2, 8))),
        "w_value": gaussian(keys[4], (D,), D ** -0.5, 0.046875, ((0, 8),), jnp.float32),
        "targets": with_ends(jax.random.randint(keys[5], (TOKENS,), -128, 128), jax.random.fold_in(keys[5], 1), -128, 127).astype(jnp.int32),
    }


EPSILON = 1e-05
GRAD_SCALE = 64.0

def silu_slope(preact):
    sigm = jax.nn.sigmoid(preact)
    return sigm * (1.0 + preact * (1.0 - sigm))

def layer_parts(inputs, gain_row, down_mat):
    floats = inputs.astype(jnp.float32)
    inv_rms = lax.rsqrt(lax.optimization_barrier(jnp.mean(floats * floats, axis=-1, keepdims=True)) + EPSILON)
    scaled = (floats * gain_row).astype(jnp.bfloat16)
    preact = inv_rms * jnp.dot(scaled, down_mat, preferred_element_type=jnp.float32)
    hidden = jax.nn.silu(preact).astype(jnp.bfloat16)
    return (floats, inv_rms, scaled, preact, hidden)

def reference(tokens, gain, w_down, w_up, w_value, targets):
    quarter = RANK // REPLICAS
    down_all = w_down.reshape(REPLICAS, LAYERS, D, quarter).transpose(1, 2, 0, 3).reshape(LAYERS, D, RANK)
    up_all = w_up.reshape(REPLICAS, LAYERS, quarter, D).transpose(1, 0, 2, 3).reshape(LAYERS, RANK, D)

    def forward_layer(inputs, params):
        gain_row, down_mat, up_mat = params
        floats, inv_rms, scaled, preact, hidden = layer_parts(inputs, gain_row, down_mat)
        output = (floats + jnp.dot(hidden, up_mat, preferred_element_type=jnp.float32)).astype(jnp.bfloat16)
        return (output, inputs)
    final_rows, saved = lax.scan(forward_layer, tokens, (gain, down_all, up_all))
    value = lax.optimization_barrier(jnp.sum(final_rows.astype(jnp.float32) * w_value, axis=-1))
    target_rows = targets.astype(jnp.float32) / 64.0
    grad_last = ((GRAD_SCALE * (value - target_rows))[:, None] * w_value).astype(jnp.bfloat16)

    def backward_layer(grad_in, params):
        gain_row, down_mat, up_mat, inputs = params
        floats, inv_rms, scaled, preact, hidden = layer_parts(inputs, gain_row, down_mat)
        grad_hidden = jnp.dot(grad_in, up_mat.T, preferred_element_type=jnp.float32)
        slope_grad = grad_hidden * silu_slope(preact)
        grad_pre = (slope_grad * inv_rms).astype(jnp.bfloat16)
        up_grad = jnp.dot(hidden.T, grad_in, preferred_element_type=jnp.float32).astype(jnp.bfloat16)
        down_grad = jnp.dot(scaled.T, grad_pre, preferred_element_type=jnp.float32).astype(jnp.bfloat16)
        grad_scaled = jnp.dot(grad_pre, down_mat.T, preferred_element_type=jnp.float32)
        inner_sum = lax.optimization_barrier(jnp.sum(slope_grad * preact, axis=-1, keepdims=True))
        grad_out = (grad_in.astype(jnp.float32) + gain_row * grad_scaled - floats * inv_rms * inv_rms * inner_sum / D).astype(jnp.bfloat16)
        return (grad_out, (down_grad, up_grad))
    grad_first, grads = lax.scan(backward_layer, grad_last, (gain, down_all, up_all, saved), reverse=True)
    down_out = grads[0].reshape(LAYERS, D, REPLICAS, quarter).transpose(2, 0, 1, 3).reshape(REPLICAS * LAYERS, D, quarter)
    up_out = grads[1].reshape(LAYERS, REPLICAS, quarter, D).transpose(1, 0, 2, 3).reshape(REPLICAS * LAYERS, quarter, D)
    return (down_out, up_out)
```

```python
import jax
import jax.numpy as jnp
from jax import lax
from jax.experimental import pallas as pl
from jax.experimental.pallas import tpu as pltpu
from jax.sharding import PartitionSpec as P

EPSILON = 1e-05
GRAD_SCALE = 64.0
BF = jnp.bfloat16
F32 = jnp.float32
SEC, TEN = "section", "tensor"
PAIRS = 4
QUARTERS = 4
CHUNK = 128
PAIR = QUARTERS * CHUNK
RANKS = PAIRS * PAIR
OWN = 32

NN = (((1,), (0,)), ((), ()))
NT = (((1,), (1,)), ((), ()))
TN = (((0,), (0,)), ((), ()))


def dot(a, b, dims):
    return lax.dot_general(a, b, dims, preferred_element_type=F32)


def flip(value, axis, mask):
    count = lax.axis_size(axis)
    return lax.ppermute(value, axis, [(i, i ^ mask) for i in range(count)])


def turn_z(value, step):
    pairs = [(i, (i // 4 + step) % 8 * 4 + i % 4) for i in range(32)]
    return lax.ppermute(value, SEC, pairs)


def turn_y(value, step):
    pairs = [(i, i // 4 * 4 + (i + step) % 4) for i in range(8)]
    return lax.ppermute(value, TEN, pairs)


def by_order(first, mine, other):
    return jnp.where(first, jnp.stack([mine, other]), jnp.stack([other, mine]))


def put(buffer, update, start):
    start = tuple(start) + (0,) * (buffer.ndim - len(start))
    return lax.dynamic_update_slice(buffer, update, start)


def gather_section(value):
    spot = lax.axis_index(SEC)
    z, x_hi = spot // 4, spot // 2 % 2
    unit = by_order(x_hi == 0, value, flip(value, SEC, 2))
    buffer = jnp.zeros((PAIRS, QUARTERS) + value.shape, value.dtype)

    def place(buffer, unit, z):
        return put(buffer, unit[:, None], (z % 2 * 2, z // 2))

    buffer = place(buffer, unit, z)
    ahead = behind = unit
    for step in (1, 2, 3):
        ahead, behind = turn_z(ahead, 1), turn_z(behind, -1)
        buffer = place(buffer, ahead, (z - step) % 8)
        buffer = place(buffer, behind, (z + step) % 8)
    far = jnp.concatenate([turn_z(ahead[:1], 1), turn_z(behind[1:], -1)])
    return place(buffer, far, (z + 4) % 8)


def gather_tensor(value):
    core = lax.axis_index(SEC) % 2
    spot = lax.axis_index(TEN)
    x_lo, y = spot // 4, spot % 4
    unit = by_order(x_lo == 0, value, flip(value, TEN, 4))
    buffer = jnp.zeros((2, 4) + value.shape, value.dtype)
    ahead, behind = turn_y(unit, 1), turn_y(unit, -1)
    far = jnp.concatenate([turn_y(ahead[:1], 1), turn_y(behind[1:], -1)])
    for piece, at in ((unit, y), (ahead, (y - 1) % 4), (behind, (y + 1) % 4), (far, (y + 2) % 4)):
        buffer = put(buffer, piece[:, None], (0, at))
    other = flip(buffer, SEC, 1)
    full = jnp.zeros((2, 4, 2) + value.shape, value.dtype)
    full = put(full, buffer[:, :, None], (0, 0, core))
    return put(full, other[:, :, None], (0, 0, 1 - core))


def two_halves(value):
    high = value.astype(BF)
    return high, (value - high.astype(F32)).astype(BF)


def sigmoid(value):
    return 1.0 / (1.0 + jnp.exp(-value))


def chain_kernel(
    c_ref, a_ref, b_ref, uw_ref, stat_ref, goal_ref, h_ref, g_ref, s_ref, pre_ref, full_ref, hs_ref
):
    lane = lax.broadcasted_iota(jnp.int32, (OWN, PAIR), 1)
    even = lane % CHUNK < CHUNK // 2
    width = 8.0 * 2048.0
    square = stat_ref[:, 0:1]
    value = stat_ref[:, 1:2]
    rms = []
    for m in range(PAIRS):
        lo, hi = m * PAIR, (m + 1) * PAIR
        rows = slice(lo, hi)
        tot = a_ref[:, rows]
        mix = b_ref[:, rows]
        if m:
            before = h_ref[:, :lo]
            tot = tot + dot(before, c_ref[:lo, rows], NN)
            mix = mix + dot(before, c_ref[rows, :lo], NT)
        own = c_ref[rows, rows]
        inv = lax.rsqrt(square / width + EPSILON)
        pre_e = inv * tot
        h_e = jnp.where(even, pre_e * sigmoid(pre_e), 0.0).astype(BF)
        step = dot(h_e, own, NN)
        h_f = h_e.astype(F32)
        square = square + jnp.sum(h_f * (2.0 * mix + step), axis=1, keepdims=True)
        full_e = mix + step
        mix = mix + dot(h_e, own, NT)
        tot = tot + step
        inv_o = lax.rsqrt(square / width + EPSILON)
        pre_o = inv_o * tot
        h_o = jnp.where(even, 0.0, pre_o * sigmoid(pre_o)).astype(BF)
        step = dot(h_o, own, NN)
        h_f = h_o.astype(F32)
        square = square + jnp.sum(h_f * (2.0 * mix + step), axis=1, keepdims=True)
        full_ref[:, rows] = jnp.where(even, full_e, mix + step)
        pre_ref[:, rows] = jnp.where(even, pre_e, pre_o)
        h_ref[:, rows] = h_e + h_o
        both = (h_e + h_o).astype(F32)
        value = value + jnp.sum(both * uw_ref[0:1, rows], axis=1, keepdims=True)
        rms.append((inv, inv_o))
    err = GRAD_SCALE * (value - goal_ref[:, 0:1])
    mark = lax.broadcasted_iota(jnp.int32, (OWN, CHUNK), 1)
    scalars = jnp.where(mark == 8, err, 0.0)
    total = jnp.zeros((OWN, 1), F32)
    for m in reversed(range(PAIRS)):
        lo, hi = m * PAIR, (m + 1) * PAIR
        rows = slice(lo, hi)
        base = err * uw_ref[0:1, rows]
        if m < PAIRS - 1:
            base = base - dot(hs_ref[:, hi:], c_ref[hi:, rows], NN)
            base = base + dot(g_ref[:, hi:], c_ref[rows, hi:], NT)
        own = c_ref[rows, rows]
        pre = pre_ref[:, rows]
        sig = sigmoid(pre)
        slope = sig * (1.0 + pre * (1.0 - sig))
        full = full_ref[:, rows]
        inv_e, inv_o = rms[m]
        h_f = h_ref[:, rows].astype(F32)
        scalars = jnp.where(mark == 2 * m + 1, total, scalars)
        grad = jnp.where(even, 0.0, (base - total * full) * slope)
        g_o = (grad * inv_o).astype(BF)
        hs_o = jnp.where(even, 0.0, total * h_f).astype(BF)
        total = total + inv_o * inv_o * jnp.sum(grad * pre, axis=1, keepdims=True) / width
        base = base - dot(hs_o, own, NN) + dot(g_o, own, NT)
        scalars = jnp.where(mark == 2 * m, total, scalars)
        grad = jnp.where(even, (base - total * full) * slope, 0.0)
        g_e = (grad * inv_e).astype(BF)
        hs_ref[:, rows] = hs_o + jnp.where(even, total * h_f, 0.0).astype(BF)
        g_ref[:, rows] = g_e + g_o
        total = total + inv_e * inv_e * jnp.sum(grad * pre, axis=1, keepdims=True) / width
    s_ref[...] = scalars


def chain(mixing, down_part, up_part, up_value, stats, goal):
    return pl.pallas_call(
        chain_kernel,
        out_shape=(
            jax.ShapeDtypeStruct((OWN, RANKS), BF),
            jax.ShapeDtypeStruct((OWN, RANKS), BF),
            jax.ShapeDtypeStruct((OWN, CHUNK), F32),
        ),
        in_specs=[pl.BlockSpec(memory_space=pltpu.VMEM)] * 6,
        out_specs=(pl.BlockSpec(memory_space=pltpu.VMEM),) * 3,
        scratch_shapes=[
            pltpu.VMEM((OWN, RANKS), F32),
            pltpu.VMEM((OWN, RANKS), F32),
            pltpu.VMEM((OWN, RANKS), BF),
        ],
        compiler_params=pltpu.CompilerParams(vmem_limit_bytes=40 * 2**20),
        name="layers",
    )(mixing, down_part, up_part, up_value, stats, goal)


def per_device(tokens, gain, w_down, w_up, w_value, targets):
    spot = lax.axis_index(SEC)
    core = spot % 2
    layer = spot % 8
    pair, quarter = layer // 2, spot // 8
    column = lax.axis_index(TEN)
    half = tokens.shape[1] // 2

    def my_half(value, axis):
        return lax.dynamic_slice_in_dim(value, core * half, half, axis)

    def their_half(value, axis):
        return lax.dynamic_slice_in_dim(value, (1 - core) * half, half, axis)

    up = w_up[0]
    down = (w_down[0].T.astype(F32) * lax.dynamic_slice_in_dim(gain, layer, 1, 0)).astype(BF)
    both = jnp.stack([up, down])
    theirs = flip(their_half(both, 2), SEC, 1)
    mine = by_order(core == 0, my_half(both, 2), theirs)
    up_two = mine[:, 0].reshape(CHUNK, half)
    down_two = mine[:, 1].reshape(CHUNK, half)
    rows = my_half(tokens, 1)
    head = my_half(w_value, 0)
    gain_two = my_half(lax.dynamic_slice_in_dim(gain, pair * 2, 2, 0), 1)

    up_all = gather_section(up_two).reshape(RANKS, half)
    down_in, _ = lax.optimization_barrier((down_two, up_all))
    down_all = gather_section(down_in).reshape(RANKS, half)

    sides = jnp.concatenate([down_two, up_two])
    wide = dot(up_all, sides, NT)
    row_layer = lax.broadcasted_iota(jnp.int32, (RANKS, CHUNK), 0)
    row_layer = row_layer // PAIR * 2 + row_layer % CHUNK // 64
    lane_layer = pair * 2 + lax.broadcasted_iota(jnp.int32, (RANKS, CHUNK), 1) // 64
    mixing = jnp.where(row_layer < lane_layer, wide[:, :CHUNK], wide[:, CHUNK:])
    entry = dot(rows, sides, NT)
    floats = rows.astype(F32)
    lane = lax.broadcasted_iota(jnp.int32, (512, CHUNK), 1)
    squares = jnp.sum(floats * floats, axis=1, keepdims=True)
    values = jnp.sum(floats * head, axis=1, keepdims=True)
    stats = jnp.where(lane == 0, squares, jnp.where(lane == 1, values, 0.0))
    up_value = jnp.sum(up_two.astype(F32) * head, axis=1)
    parts = jnp.concatenate(
        [
            mixing.reshape(8, 2, 128, CHUNK),
            entry[:, :CHUNK].reshape(8, 2, OWN, CHUNK),
            entry[:, CHUNK:].reshape(8, 2, OWN, CHUNK),
            stats.reshape(8, 2, OWN, CHUNK),
            jnp.broadcast_to(up_value, (8, 2, 8, CHUNK)),
        ],
        axis=2,
    )
    there = flip(lax.dynamic_index_in_dim(parts, 1 - core, 1, False), SEC, 1)
    sums = lax.dynamic_index_in_dim(parts, core, 1, False) + there
    sums = jnp.sum(lax.all_to_all(sums, TEN, 0, 0), axis=0)

    high, low = two_halves(jnp.concatenate([sums[128:192], sums[224:232]]))
    wide = gather_section(jnp.concatenate([sums[:128].astype(BF), high, low]))
    entry = wide[:, :, 128:200].astype(F32) + wide[:, :, 200:272].astype(F32)
    entry = entry.transpose(2, 0, 1, 3).reshape(72, RANKS)
    mixing = gather_tensor(wide[:, :, :128].reshape(16, 128, CHUNK)).reshape(16, 16, 128, CHUNK)
    mixing = mixing.transpose(0, 2, 1, 3).reshape(RANKS, RANKS)
    first = column * 64 + core * OWN
    goal = lax.dynamic_slice_in_dim(targets, first, OWN, 0).astype(F32)[:, None] / 64.0

    hidden, grad_pre, scalars = chain(
        mixing, entry[:OWN], entry[OWN : 2 * OWN], entry[2 * OWN :], sums[192:224], goal
    )

    high, low = two_halves(scalars[:, :64])
    told = gather_tensor(jnp.concatenate([hidden, grad_pre, high, low], axis=1))
    told = told.reshape(512, 2 * RANKS + CHUNK)
    hidden, grad_pre = told[:, :RANKS], told[:, RANKS : 2 * RANKS]
    scalars = told[:, 2 * RANKS :].astype(F32)
    scalars = scalars[:, :64] + scalars[:, 64:]
    err = scalars[:, 8:9]
    tail = scalars[:, :8]

    at = (pair * QUARTERS + quarter) * CHUNK
    h_own = lax.dynamic_slice_in_dim(hidden, at, CHUNK, 1)
    g_own = lax.dynamic_slice_in_dim(grad_pre, at, CHUNK, 1)
    tail_two = lax.dynamic_slice_in_dim(tail, pair * 2, 2, 1)
    tail_own = jnp.where(lane < 64, tail_two[:, 0:1], tail_two[:, 1:2])
    hs_own = (h_own.astype(F32) * tail_own).astype(BF)
    tail_all = jnp.broadcast_to(
        tail.reshape(512, PAIRS, 1, 2, 1), (512, PAIRS, QUARTERS, 2, 64)
    ).reshape(512, RANKS)
    hs_all = (hidden.astype(F32) * tail_all).astype(BF)

    col_layer = lax.broadcasted_iota(jnp.int32, (CHUNK, RANKS), 1)
    col_layer = col_layer // PAIR * 2 + col_layer % CHUNK // 64
    own_layer = pair * 2 + lax.broadcasted_iota(jnp.int32, (CHUNK, RANKS), 0) // 64
    down_mix = jnp.where(col_layer < own_layer, dot(g_own, hidden, TN), 0.0).astype(BF)
    up_mix = jnp.where(
        col_layer <= own_layer, dot(hs_own, hidden, TN), dot(h_own, hs_all, TN)
    ).astype(BF)
    top_mix = jnp.where(col_layer > own_layer, dot(h_own, grad_pre, TN), 0.0).astype(BF)

    gain_rows = jnp.broadcast_to(gain_two[:, None], (2, 64, half)).reshape(CHUNK, half)
    grad_down = gain_rows * (dot(g_own, rows, TN) + dot(down_mix, up_all, NN))
    seed = jnp.sum(h_own.astype(F32) * err, axis=0)[:, None] * head
    grad_up = (
        seed + dot(top_mix, down_all, NN) - dot(hs_own, rows, TN) - dot(up_mix, up_all, NN)
    )
    grads = jnp.stack([grad_down, grad_up]).astype(BF).reshape(2, 2, 64, half)
    theirs = flip(lax.dynamic_index_in_dim(grads, 1 - core, 1, False), SEC, 1)
    mine = lax.dynamic_index_in_dim(grads, core, 1, False)
    whole = jnp.where(
        core == 0, jnp.concatenate([mine, theirs], 2), jnp.concatenate([theirs, mine], 2)
    )
    return whole[0].T[None], whole[1][None]


def solution(mesh):
    placed = (
        P(None, TEN),
        P(None, TEN),
        P(SEC, TEN, None),
        P(SEC, None, TEN),
        P(TEN),
        P(),
    )
    return jax.shard_map(
        per_device,
        mesh=mesh,
        in_specs=placed,
        out_specs=(P(SEC, TEN, None), P(SEC, None, TEN)),
        check_vma=False,
    )
```

```python
import jax
import jax.numpy as jnp
from jax import lax
from jax.experimental import pallas as pl
from jax.experimental.pallas import tpu as pltpu
from jax.sharding import PartitionSpec as P

EPSILON = 1e-05
GRAD_SCALE = 64.0
BF = jnp.bfloat16
F32 = jnp.float32
SEC, TEN = "section", "tensor"
PAIRS = 4
QUARTERS = 4
CHUNK = 128
PAIR = QUARTERS * CHUNK
RANKS = PAIRS * PAIR
OWN = 32

NN = (((1,), (0,)), ((), ()))
NT = (((1,), (1,)), ((), ()))
TN = (((0,), (0,)), ((), ()))


def dot(a, b, dims):
    return lax.dot_general(a, b, dims, preferred_element_type=F32)


def flip(value, axis, mask):
    count = lax.axis_size(axis)
    return lax.ppermute(value, axis, [(i, i ^ mask) for i in range(count)])


def turn_z(value, step):
    pairs = [(i, (i // 4 + step) % 8 * 4 + i % 4) for i in range(32)]
    return lax.ppermute(value, SEC, pairs)


def turn_y(value, step):
    pairs = [(i, i // 4 * 4 + (i + step) % 4) for i in range(8)]
    return lax.ppermute(value, TEN, pairs)


def turn_x(value, step):
    pairs = []
    for i in range(256):
        spot, column = i // 8, i % 8
        x = (spot // 2 % 2 * 2 + column // 4 + step) % 4
        there = spot // 4 * 4 + x // 2 * 2 + spot % 2
        pairs.append((i, there * 8 + x % 2 * 4 + column % 4))
    return lax.ppermute(value, (SEC, TEN), pairs)


def by_order(first, mine, other):
    return jnp.where(first, jnp.stack([mine, other]), jnp.stack([other, mine]))


def ring_z(unit):
    ahead = behind = unit
    found = [unit]
    for _ in range(3):
        ahead, behind = turn_z(ahead, 1), turn_z(behind, -1)
        found += [ahead, behind]
    return found + [turn_z(ahead[:1], 1), turn_z(behind[1:], -1)]


REL = (0, 7, 1, 6, 2, 5, 3, 4)
ALONG_Z = [[z * 4 + i for z in range(8)] for i in range(4)]


def gather_by(value, groups):
    wide = jnp.broadcast_to(value, (len(groups[0]),) + value.shape)
    return lax.all_to_all(wide, SEC, 0, 0, axis_index_groups=groups)


def base_of(z, x_hi):
    return pl.multiple_of((z % 2 * 2 + x_hi) * PAIR + z // 2 * CHUNK, CHUNK)


def line_of(value, turn):
    return [value, turn(value, 1), turn(value, -1), turn(value, 2)]


def together(*groups):
    return lax.optimization_barrier(groups)


def shared(pieces):
    return [flip(piece, SEC, 1) for piece in pieces]


def plane(low, high):
    low, high = together(line_of(low, turn_x), line_of(high, turn_y))
    low, high = jnp.stack(low), jnp.stack(high)
    low, high = together(
        [low, turn_y(low, 1), turn_y(low, -1)], [high, turn_x(high, 1), turn_x(high, -1)]
    )
    low += [turn_y(low[1][:2], 1), turn_y(low[2][2:], -1)]
    high += [turn_x(high[1][:2], 1), turn_x(high[2][2:], -1)]
    return low + high


def columns_of(low, high):
    low, high = together([low, flip(low, TEN, 4)], line_of(high, turn_y))
    low, high = jnp.stack(low), jnp.stack(high)
    low, high = together([low, turn_y(low, 1), turn_y(low, -1)], [high, flip(high, TEN, 4)])
    return low + [turn_y(low[1][:1], 1), turn_y(low[2][1:], -1)] + high


STEPS = (0, 3, 1, 2)


def two_halves(value):
    high = value.astype(BF)
    return high, (value - high.astype(F32)).astype(BF)


def sigmoid(value):
    return 1.0 / (1.0 + jnp.exp(-value))


def chain_kernel(spot_ref, *refs):
    blocks, refs = refs[:20], refs[20:]
    entries_refs, refs = refs[:2], refs[2:]
    stat_ref, goal_ref, h_ref, g_ref, s_ref = refs[:5]
    c_ref, entry_ref, pre_ref, full_ref, hs_ref, sems = refs[5:]
    x, y, core = spot_ref[0], spot_ref[1], spot_ref[2]

    copies = []
    for index in range(20):
        odd, late = 1 - index % 10 // 5, min(index % 5, 3)
        owner = core if index < 10 else 1 - core
        first = 2 if index % 5 == 4 else 0
        ref = blocks[index]
        for at in range(ref.shape[0]):
            dy, dx = STEPS[late], STEPS[at + first]
            if odd == 0:
                dx, dy = dy, dx
            x_at, y_at = (x + dx) % 4, (y + dy) % 4
            row = pl.multiple_of(((x_at % 2 * 4 + y_at) * 2 + owner) * CHUNK, CHUNK)
            col = pl.multiple_of((odd * 2 + x_at // 2) * PAIR, PAIR)
            copies.append(
                pltpu.make_async_copy(
                    ref.at[at],
                    c_ref.at[pl.ds(row, CHUNK), pl.ds(col, PAIR)],
                    sems.at[len(copies)],
                )
            )
    for copy in copies:
        copy.start()
    for side in range(2):
        x_hi = x // 2 if side == 0 else 1 - x // 2
        for k in range(8):
            part = entries_refs[side][k].astype(F32)
            at = base_of(k, x_hi)
            entry_ref[: 2 * OWN, pl.ds(at, CHUNK)] = part[: 2 * OWN]
            head = part[64:65] + part[65:66]
            entry_ref[2 * OWN :, pl.ds(at, CHUNK)] = jnp.broadcast_to(head, (8, CHUNK))
    for copy in copies:
        copy.wait()
    a_ref, b_ref = entry_ref.at[:OWN], entry_ref.at[OWN : 2 * OWN]
    uw_ref = entry_ref.at[2 * OWN :]
    lane = lax.broadcasted_iota(jnp.int32, (OWN, PAIR), 1)
    even = lane % CHUNK < CHUNK // 2
    width = 8.0 * 2048.0
    square = jnp.broadcast_to(stat_ref[0:1, :], (CHUNK, CHUNK)).T[:OWN, 0:1]
    value = jnp.broadcast_to(stat_ref[1:2, :], (CHUNK, CHUNK)).T[:OWN, 0:1]
    rms = []
    for m in range(PAIRS):
        lo, hi = m * PAIR, (m + 1) * PAIR
        rows = slice(lo, hi)
        tot = a_ref[:, rows]
        mix = b_ref[:, rows]
        if m:
            before = h_ref[:, :lo]
            tot = tot + dot(before, c_ref[:lo, rows], NN)
            mix = mix + dot(before, c_ref[rows, :lo], NT)
        own = c_ref[rows, rows]
        inv = lax.rsqrt(square / width + EPSILON)
        pre_e = inv * tot
        h_e = jnp.where(even, pre_e * sigmoid(pre_e), 0.0).astype(BF)
        step = dot(h_e, own, NN)
        h_f = h_e.astype(F32)
        square = square + jnp.sum(h_f * (2.0 * mix + step), axis=1, keepdims=True)
        full_e = mix + step
        mix = mix + dot(h_e, own, NT)
        tot = tot + step
        inv_o = lax.rsqrt(square / width + EPSILON)
        pre_o = inv_o * tot
        h_o = jnp.where(even, 0.0, pre_o * sigmoid(pre_o)).astype(BF)
        step = dot(h_o, own, NN)
        h_f = h_o.astype(F32)
        square = square + jnp.sum(h_f * (2.0 * mix + step), axis=1, keepdims=True)
        full_ref[:, rows] = jnp.where(even, full_e, mix + step)
        pre_ref[:, rows] = jnp.where(even, pre_e, pre_o)
        h_ref[:, rows] = h_e + h_o
        both = (h_e + h_o).astype(F32)
        value = value + jnp.sum(both * uw_ref[0:1, rows], axis=1, keepdims=True)
        rms.append((inv, inv_o))
    err = GRAD_SCALE * (value - goal_ref[:, 0:1])
    mark = lax.broadcasted_iota(jnp.int32, (OWN, CHUNK), 1)
    scalars = jnp.where(mark == 8, err, 0.0)
    total = jnp.zeros((OWN, 1), F32)
    for m in reversed(range(PAIRS)):
        lo, hi = m * PAIR, (m + 1) * PAIR
        rows = slice(lo, hi)
        base = err * uw_ref[0:1, rows]
        if m < PAIRS - 1:
            base = base - dot(hs_ref[:, hi:], c_ref[hi:, rows], NN)
            base = base + dot(g_ref[:, hi:], c_ref[rows, hi:], NT)
        own = c_ref[rows, rows]
        pre = pre_ref[:, rows]
        sig = sigmoid(pre)
        slope = sig * (1.0 + pre * (1.0 - sig))
        full = full_ref[:, rows]
        inv_e, inv_o = rms[m]
        h_f = h_ref[:, rows].astype(F32)
        scalars = jnp.where(mark == 2 * m + 1, total, scalars)
        grad = jnp.where(even, 0.0, (base - total * full) * slope)
        g_o = (grad * inv_o).astype(BF)
        hs_o = jnp.where(even, 0.0, total * h_f).astype(BF)
        total = total + inv_o * inv_o * jnp.sum(grad * pre, axis=1, keepdims=True) / width
        base = base - dot(hs_o, own, NN) + dot(g_o, own, NT)
        scalars = jnp.where(mark == 2 * m, total, scalars)
        grad = jnp.where(even, (base - total * full) * slope, 0.0)
        g_e = (grad * inv_e).astype(BF)
        hs_ref[:, rows] = hs_o + jnp.where(even, total * h_f, 0.0).astype(BF)
        g_ref[:, rows] = g_e + g_o
        total = total + inv_e * inv_e * jnp.sum(grad * pre, axis=1, keepdims=True) / width
    s_ref[...] = scalars


def chain(where, blocks, entries, stats, goal):
    vmem = pl.BlockSpec(memory_space=pltpu.VMEM)
    return pl.pallas_call(
        chain_kernel,
        out_shape=(
            jax.ShapeDtypeStruct((OWN, RANKS), BF),
            jax.ShapeDtypeStruct((OWN, RANKS), BF),
            jax.ShapeDtypeStruct((OWN, CHUNK), F32),
        ),
        in_specs=[pl.BlockSpec(memory_space=pltpu.SMEM)]
        + [pl.BlockSpec(memory_space=pl.ANY)] * 20
        + [vmem] * 4,
        out_specs=(vmem,) * 3,
        scratch_shapes=[
            pltpu.VMEM((RANKS, RANKS), BF),
            pltpu.VMEM((72, RANKS), F32),
            pltpu.VMEM((OWN, RANKS), F32),
            pltpu.VMEM((OWN, RANKS), F32),
            pltpu.VMEM((OWN, RANKS), BF),
            pltpu.SemaphoreType.DMA((64,)),
        ],
        compiler_params=pltpu.CompilerParams(vmem_limit_bytes=58 * 2**20),
        name="layers",
    )(where, *blocks, *entries, stats, goal)


TOLD = 2 * RANKS + CHUNK
SHARE = OWN // 2


def gradient_kernel(spot_ref, *refs):
    blocks, units, refs = refs[:14], refs[14:23], refs[23:]
    downs_ref, rows_ref, gain_ref, head_ref, out_ref, told_ref, hs_ref = refs
    x, y, core, pair, z = [spot_ref[i] for i in range(5)]
    for index in range(14):
        owner = core if index < 7 else 1 - core
        kind = index % 7
        for place in range(blocks[index].shape[0]):
            if kind < 5:
                other, step = place + (1 if kind == 4 else 0), STEPS[min(kind, 3)]
            else:
                other, step = kind - 5, STEPS[place]
            x_lo = x % 2 if other == 0 else 1 - x % 2
            row = ((x_lo * 4 + (y + step) % 4) * 2 + owner) * OWN + kind // 5 * SHARE
            told_ref[pl.ds(pl.multiple_of(row, SHARE), SHARE), :] = blocks[index][place]
    column = base_of(z, x // 2)
    h_own = told_ref[:, pl.ds(column, CHUNK)]
    g_own = told_ref[:, pl.ds(pl.multiple_of(RANKS + column, CHUNK), CHUNK)]
    parts = told_ref[:, 2 * RANKS :]
    tail = parts.astype(F32)
    tail = tail[:, : CHUNK // 2] + tail[:, CHUNK // 2 :]
    lane = lax.broadcasted_iota(jnp.int32, (512, PAIR), 1)
    even = lane % CHUNK < CHUNK // 2
    tail_own = jnp.zeros((512, CHUNK), F32)
    for m in range(PAIRS):
        cols = slice(m * PAIR, (m + 1) * PAIR)
        scale = jnp.where(even, tail[:, 2 * m : 2 * m + 1], tail[:, 2 * m + 1 : 2 * m + 2])
        hs_ref[:, cols] = (told_ref[:, cols].astype(F32) * scale).astype(BF)
        tail_own = jnp.where(pair == m, scale[:, :CHUNK], tail_own)
    h_turn = h_own.T
    g_turn = g_own.T
    hs_turn = (h_own.astype(F32) * tail_own).astype(BF).T
    seed = dot(h_turn, parts, NN)
    seed = seed[:, 8:9] + seed[:, 72:73]
    both = jnp.concatenate([hs_turn, g_turn])
    grad_down = dot(g_turn, rows_ref[...], NN)
    grad_up = seed * head_ref[0:1, :] - dot(hs_turn, rows_ref[...], NN)
    own_layer = pair * 2 + lax.broadcasted_iota(jnp.int32, (CHUNK, 2 * CHUNK), 0) // 64
    lane = lax.broadcasted_iota(jnp.int32, (CHUNK, 2 * CHUNK), 1)
    for k in range(8):
        at = (z + REL[k]) % 8
        sides = (x // 2, 1 - x // 2)
        layer = jnp.where(lane < CHUNK, sides[0], sides[1]) * 2 + lane % CHUNK // 64
        layer = layer + at % 2 * 4

        def columns(ref, base):
            starts = [pl.multiple_of(base + base_of(at, side), CHUNK) for side in sides]
            return jnp.concatenate([ref[:, pl.ds(start, CHUNK)] for start in starts], axis=1)

        mixed = dot(both, columns(told_ref, 0), NN)
        later = dot(h_turn, columns(hs_ref, 0), NN)
        top = dot(h_turn, columns(told_ref, RANKS), NN)
        down_mix = jnp.where(layer < own_layer, mixed[CHUNK:], 0.0).astype(BF)
        up_mix = jnp.where(layer <= own_layer, mixed[:CHUNK], later).astype(BF)
        top_mix = jnp.where(layer > own_layer, top, 0.0).astype(BF)
        if k < 7:
            unit = units[k][...].reshape(2 * CHUNK, -1)
        else:
            unit = jnp.concatenate([units[7][0], units[8][0]])
        below = downs_ref[at].reshape(2 * CHUNK, -1)
        grad_down = grad_down + dot(down_mix, unit, NN)
        grad_up = grad_up - dot(up_mix, unit, NN) + dot(top_mix, below, NN)
    low_gain = lax.broadcasted_iota(jnp.int32, (CHUNK, 1), 0) < 64
    grad_down = grad_down * jnp.where(low_gain, gain_ref[0:1, :], gain_ref[1:2, :])
    for side in range(2):
        part = slice(side * 64, side * 64 + 64)
        out_ref[side, 0] = grad_down[part].astype(BF)
        out_ref[side, 1] = grad_up[part].astype(BF)


def gradients(where, blocks, units, downs, rows, gain_two, head):
    vmem = pl.BlockSpec(memory_space=pltpu.VMEM)
    half = rows.shape[1]
    return pl.pallas_call(
        gradient_kernel,
        out_shape=jax.ShapeDtypeStruct((2, 2, 64, half), BF),
        in_specs=[pl.BlockSpec(memory_space=pltpu.SMEM)] + [vmem] * 27,
        out_specs=vmem,
        scratch_shapes=[
            pltpu.VMEM((512, TOLD), BF),
            pltpu.VMEM((512, RANKS), BF),
        ],
        compiler_params=pltpu.CompilerParams(vmem_limit_bytes=48 * 2**20),
        name="gradients",
    )(where, *blocks, *units, downs, rows, gain_two, head)


SENT = CHUNK + 2 * OWN + 16


def product_kernel(spot_ref, *refs):
    units, refs = refs[:9], refs[9:]
    sides_ref, token_ref, extra_ref, mine_ref, theirs_ref, work_ref = refs
    x, core, z = spot_ref[0], spot_ref[2], spot_ref[4]
    pair = spot_ref[3]
    shape = (CHUNK, CHUNK)
    row_layer = lax.broadcasted_iota(jnp.int32, shape, 0) // 64
    lane_layer = pair * 2 + lax.broadcasted_iota(jnp.int32, shape, 1) // 64
    sides = sides_ref[...]
    for k in range(8):
        at = (z + REL[k]) % 8
        quarter = at // 2
        for side in range(2):
            x_hi = x // 2 if side == 0 else 1 - x // 2
            unit = units[k][side] if k < 7 else units[7 + side][0]
            wide = dot(unit, sides, NT)
            source = at % 2 * 2 + x_hi
            wide = jnp.where(row_layer + source * 2 < lane_layer, wide[:, :CHUNK], wide[:, CHUNK:])
            other = (quarter + core) % 2
            work_ref[other, source * 2 + quarter // 2] = wide
    blank = jnp.zeros((8, CHUNK), F32)
    for t in range(8):
        for other in range(2):
            owner = core if other == 0 else 1 - core
            row = pl.multiple_of(t * 64 + owner * OWN, OWN)
            part = token_ref[pl.ds(row, OWN), :]
            extra = extra_ref[t * 2 + owner]
            pieces = [work_ref[other, t], part[:, :CHUNK], part[:, CHUNK:]]
            pieces += [blank, extra] if other else [extra, blank]
            if other:
                theirs_ref[t] = jnp.concatenate(pieces).astype(BF)
            else:
                mine_ref[t] = jnp.concatenate(pieces)


def products(where, units, sides, tokens, extra):
    vmem = pl.BlockSpec(memory_space=pltpu.VMEM)
    return pl.pallas_call(
        product_kernel,
        out_shape=(
            jax.ShapeDtypeStruct((8, SENT, CHUNK), F32),
            jax.ShapeDtypeStruct((8, SENT, CHUNK), BF),
        ),
        in_specs=[pl.BlockSpec(memory_space=pltpu.SMEM)] + [vmem] * 12,
        out_specs=(vmem, vmem),
        scratch_shapes=[pltpu.VMEM((2, 8, CHUNK, CHUNK), F32)],
        compiler_params=pltpu.CompilerParams(vmem_limit_bytes=24 * 2**20),
        name="products",
    )(where, *units, sides, tokens, extra)


def per_device(tokens, gain, w_down, w_up, w_value, targets):
    spot = lax.axis_index(SEC)
    core = spot % 2
    layer = spot % 8
    pair = layer // 2
    column = lax.axis_index(TEN)
    half = tokens.shape[1] // 2

    def my_half(value, axis):
        return lax.dynamic_slice_in_dim(value, core * half, half, axis)

    def their_half(value, axis):
        return lax.dynamic_slice_in_dim(value, (1 - core) * half, half, axis)

    z, x_hi = spot // 4, spot // 2 % 2
    x, y = x_hi * 2 + column // 4, column % 4
    where = jnp.stack([x, y, core, pair, z]).astype(jnp.int32)

    def two_layers(value):
        theirs = flip(their_half(value, 1), SEC, 1)
        return by_order(core == 0, my_half(value, 1), theirs).reshape(CHUNK, half)

    up_far = two_layers(flip(w_up[0], SEC, 2))
    up_two = two_layers(w_up[0])
    down = w_down[0].T.astype(F32) * lax.dynamic_slice_in_dim(gain, layer, 1, 0)
    down_two = two_layers(down.astype(BF))
    rows = my_half(tokens, 1)
    head = my_half(w_value, 0)
    gain_two = my_half(lax.dynamic_slice_in_dim(gain, pair * 2, 2, 0), 1)
    units = ring_z(jnp.stack([up_two, up_far]))

    sides = jnp.concatenate([down_two, up_two])
    entry = dot(rows, sides, NT)
    floats = rows.astype(F32)
    squares = jnp.sum(floats * floats, axis=1)
    values = jnp.sum(floats * head, axis=1)
    up_value = jnp.sum(up_two.astype(F32) * head, axis=1)
    extra = [jnp.broadcast_to(up_value, (16, CHUNK))]
    extra += [jnp.pad(v.reshape(16, OWN), ((0, 0), (0, CHUNK - OWN))) for v in (squares, values)]
    extra = [part.astype(F32) for value in extra for part in two_halves(value)]
    extra = jnp.stack(extra + [jnp.zeros((16, CHUNK), F32)] * 2, axis=1)

    mine, theirs = products(where, units, sides, entry, extra)
    sums = mine + flip(theirs, SEC, 1).astype(F32)
    sums = lax.all_to_all(sums.astype(BF), TEN, 0, 0)
    sums = jnp.sum(sums.astype(F32), axis=0)
    extra = sums[192:200] + sums[200:208]
    extra = jnp.stack([extra[i] + extra[i + 1] for i in (0, 2, 4)])
    stats = jnp.pad(extra[1:], ((0, 6), (0, 0)))
    high, low = two_halves(extra[0])
    heads = jnp.pad(jnp.stack([high, low]), ((0, 14), (0, 0)))
    found = gather_by(jnp.concatenate([sums[:192].astype(BF), heads]), ALONG_Z)
    entries = found[:, CHUNK:]
    entries = [entries, flip(entries, SEC, 2)]
    found = found[:, :CHUNK].reshape(4, 2, CHUNK, CHUNK)
    evens = jnp.concatenate([found[i, 0] for i in range(4)], axis=1)
    odds = jnp.concatenate([found[i, 1] for i in range(4)], axis=1)
    blocks = plane(odds, evens)
    first = column * 64 + core * OWN
    goal = lax.dynamic_slice_in_dim(targets, first, OWN, 0).astype(F32)[:, None] / 64.0

    hidden, grad_pre, scalars = chain(where, blocks + shared(blocks), entries, stats, goal)

    downs = jnp.stack([down_two, flip(down_two, SEC, 2)])
    downs, _ = lax.optimization_barrier((downs, evens))
    downs = gather_by(downs, ALONG_Z)

    high, low = two_halves(scalars[:, : CHUNK // 2])
    told = jnp.concatenate([hidden, grad_pre, high, low], axis=1)
    blocks = columns_of(told[:SHARE], told[SHARE:])
    grads = gradients(
        where, blocks + shared(blocks), units, downs, rows, gain_two, head[None]
    )
    theirs = flip(lax.dynamic_index_in_dim(grads, 1 - core, 0, False), SEC, 1)
    mine = lax.dynamic_index_in_dim(grads, core, 0, False)
    whole = jnp.where(
        core == 0, jnp.concatenate([mine, theirs], 2), jnp.concatenate([theirs, mine], 2)
    )
    return whole[0].T[None], whole[1][None]


def solution(mesh):
    placed = (
        P(None, TEN),
        P(None, TEN),
        P(SEC, TEN, None),
        P(SEC, None, TEN),
        P(TEN),
        P(),
    )
    return jax.shard_map(
        per_device,
        mesh=mesh,
        in_specs=placed,
        out_specs=(P(SEC, TEN, None), P(SEC, None, TEN)),
        check_vma=False,
    )
```

```python
import jax
import jax.numpy as jnp
from jax import lax
from jax.experimental import pallas as pl
from jax.experimental.pallas import tpu as pltpu
from jax.sharding import PartitionSpec as P

EPSILON = 1e-05
GRAD_SCALE = 64.0
BF = jnp.bfloat16
F32 = jnp.float32
SEC, TEN = "section", "tensor"
PAIRS = 4
QUARTERS = 4
CHUNK = 128
PAIR = QUARTERS * CHUNK
RANKS = PAIRS * PAIR
OWN = 32

NN = (((1,), (0,)), ((), ()))
NT = (((1,), (1,)), ((), ()))
TN = (((0,), (0,)), ((), ()))


def dot(a, b, dims):
    return lax.dot_general(a, b, dims, preferred_element_type=F32)


def flip(value, axis, mask):
    count = lax.axis_size(axis)
    return lax.ppermute(value, axis, [(i, i ^ mask) for i in range(count)])


def turn_z(value, step):
    pairs = [(i, (i // 4 + step) % 8 * 4 + i % 4) for i in range(32)]
    return lax.ppermute(value, SEC, pairs)


def turn_y(value, step):
    pairs = [(i, i // 4 * 4 + (i + step) % 4) for i in range(8)]
    return lax.ppermute(value, TEN, pairs)


def turn_x(value, step):
    pairs = []
    for i in range(256):
        spot, column = i // 8, i % 8
        x = (spot // 2 % 2 * 2 + column // 4 + step) % 4
        there = spot // 4 * 4 + x // 2 * 2 + spot % 2
        pairs.append((i, there * 8 + x % 2 * 4 + column % 4))
    return lax.ppermute(value, (SEC, TEN), pairs)


def by_order(first, mine, other):
    return jnp.where(first, jnp.stack([mine, other]), jnp.stack([other, mine]))


def ring_z(unit):
    ahead = behind = unit
    found = [unit]
    for _ in range(3):
        ahead, behind = turn_z(ahead, 1), turn_z(behind, -1)
        found += [ahead, behind]
    return found + [turn_z(ahead[:1], 1), turn_z(behind[1:], -1)]


REL = (0, 7, 1, 6, 2, 5, 3, 4)
ALONG_Z = [[z * 4 + i for z in range(8)] for i in range(4)]


def gather_by(value, groups):
    wide = jnp.broadcast_to(value, (len(groups[0]),) + value.shape)
    return lax.all_to_all(wide, SEC, 0, 0, axis_index_groups=groups)


def base_of(z, x_hi):
    return pl.multiple_of((z % 2 * 2 + x_hi) * PAIR + z // 2 * CHUNK, CHUNK)


def line_of(value, turn):
    return [value, turn(value, 1), turn(value, -1), turn(value, 2)]


def together(*groups):
    return lax.optimization_barrier(groups)


def shared(pieces):
    return [flip(piece, SEC, 1) for piece in pieces]


def plane(low, high):
    low, high = together(line_of(low, turn_x), line_of(high, turn_y))
    low, high = jnp.stack(low), jnp.stack(high)
    line = low
    low, high = together(
        [low, turn_y(low, 1), turn_y(low, -1)], [high, turn_x(high, 1), turn_x(high, -1)]
    )
    low += [turn_y(low[1][:2], 1), turn_y(low[2][2:], -1)]
    high += [turn_x(high[1][:2], 1), turn_x(high[2][2:], -1)]
    return low + high, line


def columns_of(low, high):
    low, high = together([low, flip(low, TEN, 4)], line_of(high, turn_y))
    low, high = jnp.stack(low), jnp.stack(high)
    low, high = together([low, turn_y(low, 1), turn_y(low, -1)], [high, flip(high, TEN, 4)])
    return low + [turn_y(low[1][:1], 1), turn_y(low[2][1:], -1)] + high


STEPS = (0, 3, 1, 2)


def two_halves(value):
    high = value.astype(BF)
    return high, (value - high.astype(F32)).astype(BF)


def sigmoid(value):
    return 1.0 / (1.0 + jnp.exp(-value))


def chain_kernel(spot_ref, *refs):
    blocks, refs = refs[:20], refs[20:]
    entries_refs, refs = refs[:2], refs[2:]
    stat_ref, goal_ref, h_ref, g_ref, s_ref = refs[:5]
    c_ref, entry_ref, pre_ref, full_ref, hs_ref, sems = refs[5:]
    x, y, core = spot_ref[0], spot_ref[1], spot_ref[2]

    copies = []
    for index in range(20):
        odd, late = 1 - index % 10 // 5, min(index % 5, 3)
        owner = core if index < 10 else 1 - core
        first = 2 if index % 5 == 4 else 0
        ref = blocks[index]
        for at in range(ref.shape[0]):
            dy, dx = STEPS[late], STEPS[at + first]
            if odd == 0:
                dx, dy = dy, dx
            x_at, y_at = (x + dx) % 4, (y + dy) % 4
            row = pl.multiple_of(((x_at % 2 * 4 + y_at) * 2 + owner) * CHUNK, CHUNK)
            col = pl.multiple_of((odd * 2 + x_at // 2) * PAIR, PAIR)
            copies.append(
                pltpu.make_async_copy(
                    ref.at[at],
                    c_ref.at[pl.ds(row, CHUNK), pl.ds(col, PAIR)],
                    sems.at[len(copies)],
                )
            )
    for copy in copies:
        copy.start()
    for side in range(2):
        x_hi = x // 2 if side == 0 else 1 - x // 2
        for k in range(8):
            part = entries_refs[side][k].astype(F32)
            at = base_of(k, x_hi)
            entry_ref[: 2 * OWN, pl.ds(at, CHUNK)] = part[: 2 * OWN]
            head = part[64:65] + part[65:66]
            entry_ref[2 * OWN :, pl.ds(at, CHUNK)] = jnp.broadcast_to(head, (8, CHUNK))
    for copy in copies:
        copy.wait()
    a_ref, b_ref = entry_ref.at[:OWN], entry_ref.at[OWN : 2 * OWN]
    uw_ref = entry_ref.at[2 * OWN :]
    lane = lax.broadcasted_iota(jnp.int32, (OWN, PAIR), 1)
    even = lane % CHUNK < CHUNK // 2
    width = 8.0 * 2048.0
    square = jnp.broadcast_to(stat_ref[0:1, :], (CHUNK, CHUNK)).T[:OWN, 0:1]
    value = jnp.broadcast_to(stat_ref[1:2, :], (CHUNK, CHUNK)).T[:OWN, 0:1]
    rms = []
    for m in range(PAIRS):
        lo, hi = m * PAIR, (m + 1) * PAIR
        rows = slice(lo, hi)
        tot = a_ref[:, rows]
        mix = b_ref[:, rows]
        if m:
            before = h_ref[:, :lo]
            tot = tot + dot(before, c_ref[:lo, rows], NN)
            mix = mix + dot(before, c_ref[rows, :lo], NT)
        own = c_ref[rows, rows]
        inv = lax.rsqrt(square / width + EPSILON)
        pre_e = inv * tot
        h_e = jnp.where(even, pre_e * sigmoid(pre_e), 0.0).astype(BF)
        step = dot(h_e, own, NN)
        h_f = h_e.astype(F32)
        square = square + jnp.sum(h_f * (2.0 * mix + step), axis=1, keepdims=True)
        full_e = mix + step
        mix = mix + dot(h_e, own, NT)
        tot = tot + step
        inv_o = lax.rsqrt(square / width + EPSILON)
        pre_o = inv_o * tot
        h_o = jnp.where(even, 0.0, pre_o * sigmoid(pre_o)).astype(BF)
        step = dot(h_o, own, NN)
        h_f = h_o.astype(F32)
        square = square + jnp.sum(h_f * (2.0 * mix + step), axis=1, keepdims=True)
        full_ref[:, rows] = jnp.where(even, full_e, mix + step)
        pre_ref[:, rows] = jnp.where(even, pre_e, pre_o)
        h_ref[:, rows] = h_e + h_o
        both = (h_e + h_o).astype(F32)
        value = value + jnp.sum(both * uw_ref[0:1, rows], axis=1, keepdims=True)
        rms.append((inv, inv_o))
    err = GRAD_SCALE * (value - goal_ref[:, 0:1])
    mark = lax.broadcasted_iota(jnp.int32, (OWN, CHUNK), 1)
    scalars = jnp.where(mark == 8, err, 0.0)
    total = jnp.zeros((OWN, 1), F32)
    for m in reversed(range(PAIRS)):
        lo, hi = m * PAIR, (m + 1) * PAIR
        rows = slice(lo, hi)
        base = err * uw_ref[0:1, rows]
        if m < PAIRS - 1:
            base = base - dot(hs_ref[:, hi:], c_ref[hi:, rows], NN)
            base = base + dot(g_ref[:, hi:], c_ref[rows, hi:], NT)
        own = c_ref[rows, rows]
        pre = pre_ref[:, rows]
        sig = sigmoid(pre)
        slope = sig * (1.0 + pre * (1.0 - sig))
        full = full_ref[:, rows]
        inv_e, inv_o = rms[m]
        h_f = h_ref[:, rows].astype(F32)
        scalars = jnp.where(mark == 2 * m + 1, total, scalars)
        grad = jnp.where(even, 0.0, (base - total * full) * slope)
        g_o = (grad * inv_o).astype(BF)
        hs_o = jnp.where(even, 0.0, total * h_f).astype(BF)
        total = total + inv_o * inv_o * jnp.sum(grad * pre, axis=1, keepdims=True) / width
        base = base - dot(hs_o, own, NN) + dot(g_o, own, NT)
        scalars = jnp.where(mark == 2 * m, total, scalars)
        grad = jnp.where(even, (base - total * full) * slope, 0.0)
        g_e = (grad * inv_e).astype(BF)
        hs_ref[:, rows] = hs_o + jnp.where(even, total * h_f, 0.0).astype(BF)
        g_ref[:, rows] = g_e + g_o
        total = total + inv_e * inv_e * jnp.sum(grad * pre, axis=1, keepdims=True) / width
    s_ref[...] = scalars


def chain(where, blocks, entries, stats, goal):
    vmem = pl.BlockSpec(memory_space=pltpu.VMEM)
    return pl.pallas_call(
        chain_kernel,
        out_shape=(
            jax.ShapeDtypeStruct((OWN, RANKS), BF),
            jax.ShapeDtypeStruct((OWN, RANKS), BF),
            jax.ShapeDtypeStruct((OWN, CHUNK), F32),
        ),
        in_specs=[pl.BlockSpec(memory_space=pltpu.SMEM)]
        + [pl.BlockSpec(memory_space=pl.ANY)] * 20
        + [vmem] * 4,
        out_specs=(vmem,) * 3,
        scratch_shapes=[
            pltpu.VMEM((RANKS, RANKS), BF),
            pltpu.VMEM((72, RANKS), F32),
            pltpu.VMEM((OWN, RANKS), F32),
            pltpu.VMEM((OWN, RANKS), F32),
            pltpu.VMEM((OWN, RANKS), BF),
            pltpu.SemaphoreType.DMA((64,)),
        ],
        compiler_params=pltpu.CompilerParams(vmem_limit_bytes=58 * 2**20),
        name="layers",
    )(where, *blocks, *entries, stats, goal)


TOLD = 2 * RANKS + CHUNK
SHARE = OWN // 2


def gradient_kernel(spot_ref, *refs):
    blocks, units, refs = refs[:14], refs[14:23], refs[23:]
    downs_ref, rows_ref, gain_ref, head_ref, out_ref, told_ref, hs_ref = refs
    x, y, core, pair, z = [spot_ref[i] for i in range(5)]
    for index in range(14):
        owner = core if index < 7 else 1 - core
        kind = index % 7
        for place in range(blocks[index].shape[0]):
            if kind < 5:
                other, step = place + (1 if kind == 4 else 0), STEPS[min(kind, 3)]
            else:
                other, step = kind - 5, STEPS[place]
            x_lo = x % 2 if other == 0 else 1 - x % 2
            row = ((x_lo * 4 + (y + step) % 4) * 2 + owner) * OWN + kind // 5 * SHARE
            told_ref[pl.ds(pl.multiple_of(row, SHARE), SHARE), :] = blocks[index][place]
    column = base_of(z, x // 2)
    h_own = told_ref[:, pl.ds(column, CHUNK)]
    g_own = told_ref[:, pl.ds(pl.multiple_of(RANKS + column, CHUNK), CHUNK)]
    parts = told_ref[:, 2 * RANKS :]
    tail = parts.astype(F32)
    tail = tail[:, : CHUNK // 2] + tail[:, CHUNK // 2 :]
    lane = lax.broadcasted_iota(jnp.int32, (512, PAIR), 1)
    even = lane % CHUNK < CHUNK // 2
    tail_own = jnp.zeros((512, CHUNK), F32)
    for m in range(PAIRS):
        cols = slice(m * PAIR, (m + 1) * PAIR)
        scale = jnp.where(even, tail[:, 2 * m : 2 * m + 1], tail[:, 2 * m + 1 : 2 * m + 2])
        hs_ref[:, cols] = (told_ref[:, cols].astype(F32) * scale).astype(BF)
        tail_own = jnp.where(pair == m, scale[:, :CHUNK], tail_own)
    h_turn = h_own.T
    g_turn = g_own.T
    hs_turn = (h_own.astype(F32) * tail_own).astype(BF).T
    seed = dot(h_turn, parts, NN)
    seed = seed[:, 8:9] + seed[:, 72:73]
    both = jnp.concatenate([hs_turn, g_turn])
    grad_down = dot(g_turn, rows_ref[...], NN)
    grad_up = seed * head_ref[0:1, :] - dot(hs_turn, rows_ref[...], NN)
    own_layer = pair * 2 + lax.broadcasted_iota(jnp.int32, (CHUNK, 2 * CHUNK), 0) // 64
    lane = lax.broadcasted_iota(jnp.int32, (CHUNK, 2 * CHUNK), 1)
    for k in range(8):
        at = (z + REL[k]) % 8
        sides = (x // 2, 1 - x // 2)
        layer = jnp.where(lane < CHUNK, sides[0], sides[1]) * 2 + lane % CHUNK // 64
        layer = layer + at % 2 * 4

        def columns(ref, base):
            starts = [pl.multiple_of(base + base_of(at, side), CHUNK) for side in sides]
            return jnp.concatenate([ref[:, pl.ds(start, CHUNK)] for start in starts], axis=1)

        mixed = dot(both, columns(told_ref, 0), NN)
        later = dot(h_turn, columns(hs_ref, 0), NN)
        top = dot(h_turn, columns(told_ref, RANKS), NN)
        down_mix = jnp.where(layer < own_layer, mixed[CHUNK:], 0.0).astype(BF)
        up_mix = jnp.where(layer <= own_layer, mixed[:CHUNK], later).astype(BF)
        top_mix = jnp.where(layer > own_layer, top, 0.0).astype(BF)
        if k < 7:
            unit = units[k][...].reshape(2 * CHUNK, -1)
        else:
            unit = jnp.concatenate([units[7][0], units[8][0]])
        below = downs_ref[at].reshape(2 * CHUNK, -1)
        grad_down = grad_down + dot(down_mix, unit, NN)
        grad_up = grad_up - dot(up_mix, unit, NN) + dot(top_mix, below, NN)
    low_gain = lax.broadcasted_iota(jnp.int32, (CHUNK, 1), 0) < 64
    grad_down = grad_down * jnp.where(low_gain, gain_ref[0:1, :], gain_ref[1:2, :])
    for side in range(2):
        part = slice(side * 64, side * 64 + 64)
        out_ref[side, 0] = grad_down[part].astype(BF)
        out_ref[side, 1] = grad_up[part].astype(BF)


def gradients(where, blocks, units, downs, rows, gain_two, head):
    vmem = pl.BlockSpec(memory_space=pltpu.VMEM)
    half = rows.shape[1]
    return pl.pallas_call(
        gradient_kernel,
        out_shape=jax.ShapeDtypeStruct((2, 2, 64, half), BF),
        in_specs=[pl.BlockSpec(memory_space=pltpu.SMEM)] + [vmem] * 27,
        out_specs=vmem,
        scratch_shapes=[
            pltpu.VMEM((512, TOLD), BF),
            pltpu.VMEM((512, RANKS), BF),
        ],
        compiler_params=pltpu.CompilerParams(vmem_limit_bytes=48 * 2**20),
        name="gradients",
    )(where, *blocks, *units, downs, rows, gain_two, head)


SENT = CHUNK + 2 * OWN + 16


def product_kernel(spot_ref, *refs):
    units, refs = refs[:9], refs[9:]
    sides_ref, token_ref, extra_ref, mine_ref, theirs_ref, work_ref = refs
    x, core, z = spot_ref[0], spot_ref[2], spot_ref[4]
    pair = spot_ref[3]
    shape = (CHUNK, CHUNK)
    row_layer = lax.broadcasted_iota(jnp.int32, shape, 0) // 64
    lane_layer = pair * 2 + lax.broadcasted_iota(jnp.int32, shape, 1) // 64
    sides = sides_ref[...]
    for k in range(8):
        at = (z + REL[k]) % 8
        quarter = at // 2
        for side in range(2):
            x_hi = x // 2 if side == 0 else 1 - x // 2
            unit = units[k][side] if k < 7 else units[7 + side][0]
            wide = dot(unit, sides, NT)
            source = at % 2 * 2 + x_hi
            wide = jnp.where(row_layer + source * 2 < lane_layer, wide[:, :CHUNK], wide[:, CHUNK:])
            other = (quarter + core) % 2
            work_ref[other, source * 2 + quarter // 2] = wide
    blank = jnp.zeros((8, CHUNK), F32)
    for t in range(8):
        for other in range(2):
            owner = core if other == 0 else 1 - core
            row = pl.multiple_of(t * 64 + owner * OWN, OWN)
            part = token_ref[pl.ds(row, OWN), :]
            extra = extra_ref[t * 2 + owner]
            pieces = [work_ref[other, t], part[:, :CHUNK], part[:, CHUNK:]]
            pieces += [blank, extra] if other else [extra, blank]
            if other:
                theirs_ref[t] = jnp.concatenate(pieces).astype(BF)
            else:
                mine_ref[t] = jnp.concatenate(pieces)


def products(where, units, sides, tokens, extra):
    vmem = pl.BlockSpec(memory_space=pltpu.VMEM)
    return pl.pallas_call(
        product_kernel,
        out_shape=(
            jax.ShapeDtypeStruct((8, SENT, CHUNK), F32),
            jax.ShapeDtypeStruct((8, SENT, CHUNK), BF),
        ),
        in_specs=[pl.BlockSpec(memory_space=pltpu.SMEM)] + [vmem] * 12,
        out_specs=(vmem, vmem),
        scratch_shapes=[pltpu.VMEM((2, 8, CHUNK, CHUNK), F32)],
        compiler_params=pltpu.CompilerParams(vmem_limit_bytes=24 * 2**20),
        name="products",
    )(where, *units, sides, tokens, extra)


def per_device(tokens, gain, w_down, w_up, w_value, targets):
    spot = lax.axis_index(SEC)
    core = spot % 2
    layer = spot % 8
    pair = layer // 2
    column = lax.axis_index(TEN)
    half = tokens.shape[1] // 2

    def my_half(value, axis):
        return lax.dynamic_slice_in_dim(value, core * half, half, axis)

    def their_half(value, axis):
        return lax.dynamic_slice_in_dim(value, (1 - core) * half, half, axis)

    z, x_hi = spot // 4, spot // 2 % 2
    x, y = x_hi * 2 + column // 4, column % 4
    where = jnp.stack([x, y, core, pair, z]).astype(jnp.int32)

    def two_layers(value):
        theirs = flip(their_half(value, 1), SEC, 1)
        return by_order(core == 0, my_half(value, 1), theirs).reshape(CHUNK, half)

    up_far = two_layers(flip(w_up[0], SEC, 2))
    up_two = two_layers(w_up[0])
    down = w_down[0].T.astype(F32) * lax.dynamic_slice_in_dim(gain, layer, 1, 0)
    down_two = two_layers(down.astype(BF))
    rows = my_half(tokens, 1)
    head = my_half(w_value, 0)
    gain_two = my_half(lax.dynamic_slice_in_dim(gain, pair * 2, 2, 0), 1)
    units = ring_z(jnp.stack([up_two, up_far]))

    sides = jnp.concatenate([down_two, up_two])
    entry = dot(rows, sides, NT)
    floats = rows.astype(F32)
    squares = jnp.sum(floats * floats, axis=1)
    values = jnp.sum(floats * head, axis=1)
    up_value = jnp.sum(up_two.astype(F32) * head, axis=1)
    extra = [jnp.broadcast_to(up_value, (16, CHUNK))]
    extra += [jnp.pad(v.reshape(16, OWN), ((0, 0), (0, CHUNK - OWN))) for v in (squares, values)]
    extra = [part.astype(F32) for value in extra for part in two_halves(value)]
    extra = jnp.stack(extra + [jnp.zeros((16, CHUNK), F32)] * 2, axis=1)

    mine, theirs = products(where, units, sides, entry, extra)
    sums = mine + flip(theirs, SEC, 1).astype(F32)
    sums = lax.all_to_all(sums.astype(BF), TEN, 0, 0)
    sums = jnp.sum(sums.astype(F32), axis=0)
    extra = sums[192:200] + sums[200:208]
    extra = jnp.stack([extra[i] + extra[i + 1] for i in (0, 2, 4)])
    stats = jnp.pad(extra[1:], ((0, 6), (0, 0)))
    high, low = two_halves(extra[0])
    heads = jnp.pad(jnp.stack([high, low]), ((0, 14), (0, 0)))
    found = gather_by(jnp.concatenate([sums[:192].astype(BF), heads]), ALONG_Z)
    entries = found[:, CHUNK:]
    entries = [entries, flip(entries, SEC, 2)]
    found = found[:, :CHUNK].reshape(4, 2, CHUNK, CHUNK)
    evens = jnp.concatenate([found[i, 0] for i in range(4)], axis=1)
    odds = jnp.concatenate([found[i, 1] for i in range(4)], axis=1)
    blocks, line = plane(odds, evens)
    first = column * 64 + core * OWN
    goal = lax.dynamic_slice_in_dim(targets, first, OWN, 0).astype(F32)[:, None] / 64.0

    hidden, grad_pre, scalars = chain(where, blocks + shared(blocks), entries, stats, goal)

    downs = jnp.stack([down_two, flip(down_two, SEC, 2)])
    downs = lax.optimization_barrier(jnp.broadcast_to(downs, (8,) + downs.shape))
    downs, _ = lax.optimization_barrier((downs, line))
    downs = lax.all_to_all(downs, SEC, 0, 0, axis_index_groups=ALONG_Z)

    high, low = two_halves(scalars[:, : CHUNK // 2])
    told = jnp.concatenate([hidden, grad_pre, high, low], axis=1)
    blocks = columns_of(told[:SHARE], told[SHARE:])
    grads = gradients(
        where, blocks + shared(blocks), units, downs, rows, gain_two, head[None]
    )
    theirs = flip(lax.dynamic_index_in_dim(grads, 1 - core, 0, False), SEC, 1)
    mine = lax.dynamic_index_in_dim(grads, core, 0, False)
    whole = jnp.where(
        core == 0, jnp.concatenate([mine, theirs], 2), jnp.concatenate([theirs, mine], 2)
    )
    return whole[0].T[None], whole[1][None]


def solution(mesh):
    placed = (
        P(None, TEN),
        P(None, TEN),
        P(SEC, TEN, None),
        P(SEC, None, TEN),
        P(TEN),
        P(),
    )
    return jax.shard_map(
        per_device,
        mesh=mesh,
        in_specs=placed,
        out_specs=(P(SEC, TEN, None), P(SEC, None, TEN)),
        check_vma=False,
    )
```
